128 devices in a mesh: obs: 16 (over z, x), par: 8 (over y, core).
Axes of the slice: x: 4, y: 4, z: 4, core: 2. Of those that a mesh axis runs over, the one named last changes fastest.
Arguments:
- green: bfloat16 [65536, 16384], P('obs', 'par'), may hold values from -0.046875 to 0.046875
- blocks: int32 [512, 128], P('obs', 'par'), may hold values 0 or 1
- probes: bfloat16 [16384, 256], P('par'), may hold values from -6 to 6
- stations: int32 [65536], P(('obs', 'par')), may hold values from 0 to 127, as said below
- decay: float32 [128], P(('obs', 'par')), may hold values from 0.3 to 0.95
- noise_scale: float32 [128], P(('obs', 'par')), may hold values from 0.5 to 2
Outputs:
- sketch: float32 [256, 16384], P('obs', 'par')
The draws below stay inside these ranges and needn't reach their ends.
Inputs may be any that keep to these rules, and one draw needn't show every extreme that they name: `stations`: within each device's aligned block of 512 rows no station appears more than 8 times, and one station appears exactly 8 times in every block.
All inputs are finite; a program needn't handle non-finite values. No bound on the sum of `blocks` on one device may be relied on, other than what follows from the above.
Results may differ from the reference program's by a relative error of at most 0.0025.
Values may be sent and summed in bfloat16 or wider, within the bound.
No kernel may reach another device: no remote copies, remote signals or barrier semaphores. Data moves between devices by JAX's collectives and lax.ppermute only.
A program may use at most 128 MiB of HBM per device.

```python
import math
import jax
import jax.numpy as jnp
from jax import lax

K = 256
BLK = 128
ROWS_BLK = 512
PAR_DEV = 2048
NOBS = 65536
NPAR = 16384
STATIONS = 128
MOST = 8
N_PAR = 8
DEVICES = 128


def draw_stations(key, part):
    pool_size = DEVICES * MOST
    busiest = jax.random.randint(jax.random.fold_in(key, 7), (), 0, DEVICES)
    slot_owner = jnp.arange(pool_size, dtype=jnp.int32) // MOST

    def one_block(block_key):
        first_key, second_key = jax.random.split(block_key)
        scores = jax.random.permutation(first_key, pool_size).astype(jnp.int32) + 1
        scores = jnp.where(slot_owner == busiest, jnp.arange(pool_size, dtype=jnp.int32) - pool_size, scores)
        chosen = jnp.argsort(scores, stable=True)[:ROWS_BLK].astype(jnp.int32) // MOST
        return jax.random.permutation(second_key, chosen)
    block_keys = jax.random.split(jax.random.fold_in(key, 11), DEVICES)
    return jax.vmap(one_block)(block_keys).reshape(-1).astype(jnp.int32)


def with_ends(values, rng, low, high):
    dims = values.shape
    spot = [jax.random.randint(jax.random.fold_in(rng, axis), (), 0, dims[axis]) for axis in range(len(dims))]
    values = values.at[tuple(spot)].set(low)
    longest = dims.index(max(dims))
    spot[longest] = (spot[longest] + 1) % dims[longest]
    return values.at[tuple(spot)].set(high)


def level_of(own_key, extent, cuts, low, top_value):
    def one(position, blocks):
        heights = jax.random.uniform(jax.random.fold_in(jax.random.fold_in(own_key, 6), position), (blocks,), jnp.float32, low / len(cuts), top_value / len(cuts))
        return jnp.repeat(jnp.exp(heights), extent[position] // blocks).reshape((-1,) + (1,) * (len(extent) - position - 1))

    factor_of = one(*cuts[0])
    for cut in cuts[1:]:
        factor_of = factor_of * one(*cut)
    return factor_of


def bell_draw(stream_key, shape, deviation, bound, shards=(), kind=jnp.bfloat16):
    gain = level_of(stream_key, shape, shards, -0.22, 0.18) if shards else 1.0
    result = jax.random.normal(stream_key, shape, jnp.float32) * deviation * gain
    return jnp.minimum(jnp.maximum(result, -bound), bound).astype(kind)


def setup_inputs(seed: int = 0) -> dict:
    keys = jax.random.split(jax.random.key(seed), 7)
    return {
        "green": bell_draw(keys[0], (NOBS, NPAR), NPAR ** -0.5, 0.046875, ((0, 16), (1, 8))),
        "blocks": with_ends((jax.random.randint(keys[1], (NOBS // BLK, NPAR // BLK), 0, 4) < 3).astype(jnp.int32), jax.random.fold_in(keys[1], 1), 0, 1),
        "probes": bell_draw(keys[2], (NPAR, K), 1.0, 6.0, ((0, 8),)),
        "stations": draw_stations(jax.random.fold_in(keys[6], 71), 0),
        "decay": jnp.clip(jnp.exp(math.log(0.95) - 1.1526795 * jax.random.uniform(keys[4], (STATIONS,), jnp.float32) ** level_of(keys[4], (STATIONS,), ((0, 128),), -0.2, 0.2)), 0.3, 0.95),
        "noise_scale": jnp.clip(jnp.exp(math.log(2.0) - 1.3862944 * jax.random.uniform(keys[5], (STATIONS,), jnp.float32) ** level_of(keys[5], (STATIONS,), ((0, 128),), -0.2, 0.2)), 0.5, 2.0),
    }


def masked_tile(green, block_gate, tile_index):
    column_start = (tile_index * PAR_DEV).astype(jnp.int32)
    gate_start = (tile_index * (PAR_DEV // BLK)).astype(jnp.int32)
    green_tile = lax.dynamic_slice_in_dim(green, column_start, PAR_DEV, 1)
    gate_tile = lax.dynamic_slice_in_dim(block_gate, gate_start, PAR_DEV // BLK, 1)
    shaped = green_tile.reshape(NOBS // BLK, BLK, PAR_DEV // BLK, BLK) * gate_tile[:, None, :, None]
    return shaped.reshape(NOBS, PAR_DEV)

def reference(green, blocks, probes, stations, decay, noise_scale):
    block_gate = blocks.astype(jnp.bfloat16)

    def forward_step(tile_index, accum_sum):
        tile_probes = lax.dynamic_slice_in_dim(probes, (tile_index * PAR_DEV).astype(jnp.int32), PAR_DEV, 0)
        partial_value = jnp.dot(masked_tile(green, block_gate, tile_index), tile_probes, preferred_element_type=jnp.float32)
        return accum_sum + partial_value
    forward = lax.fori_loop(0, N_PAR, forward_step, jnp.zeros((NOBS, K), jnp.float32)).astype(jnp.bfloat16)
    order = jnp.argsort(stations, stable=True).astype(jnp.int32)
    sorted_ids = stations[order]
    sorted_rows = forward[order].astype(jnp.float32)
    same_link = sorted_ids[1:] == sorted_ids[:-1]
    same_prev = jnp.concatenate([jnp.zeros((1,), bool), same_link])
    same_next = jnp.concatenate([same_link, jnp.zeros((1,), bool)])
    rate = decay[sorted_ids][:, None]
    level = noise_scale[sorted_ids][:, None]
    stationary = jnp.sqrt(1.0 - rate * rate)
    zero_row = jnp.zeros((1, K), sorted_rows.dtype)
    prior_rows = jnp.concatenate([zero_row, sorted_rows[:-1]])
    whitened = jnp.where(same_prev[:, None], sorted_rows - rate * prior_rows, stationary * sorted_rows) / level
    following = jnp.where(same_next[:, None], jnp.concatenate([whitened[1:], zero_row]), 0.0)
    leading = jnp.where(same_prev[:, None], 1.0, stationary)
    precision_sorted = ((leading * whitened - rate * following) / level).astype(jnp.bfloat16)
    precision_rows = jnp.zeros((NOBS, K), jnp.bfloat16).at[order].set(precision_sorted)

    def adjoint_tile(tile_index):
        return lax.dot_general(precision_rows, masked_tile(green, block_gate, tile_index), (((0,), (0,)), ((), ())), preferred_element_type=jnp.float32)
    tiles = lax.map(adjoint_tile, jnp.arange(N_PAR, dtype=jnp.int32))
    return jnp.transpose(tiles, (1, 0, 2)).reshape(K, NPAR)
```

```python
import functools

import jax
import jax.numpy as jnp
from jax import lax
from jax.experimental import pallas as pl
from jax.experimental.pallas import tpu as pltpu
from jax.sharding import PartitionSpec as P

BLK = 128
CH = 256
AUG = 48
COLS = 32
BF = jnp.bfloat16
F32 = jnp.float32
NT = (((1,), (1,)), ((), ()))
MB = 1 << 20


def vm(mib):
    return pltpu.CompilerParams(vmem_limit_bytes=mib * MB)


def forward_kernel(idx, green, gate, probes, mine, send, acc):
    core = idx[0]
    parts = [green[r * BLK : (r + 1) * BLK, :] * gate[r].astype(BF) for r in range(4)]
    masked = jnp.concatenate(parts, axis=0)
    out = jnp.dot(masked, probes[...], preferred_element_type=F32)
    acc[...] = out.T
    mine[...] = acc[pl.ds(pl.multiple_of(core * 128, 128), 128), :]
    send[...] = acc[pl.ds(pl.multiple_of((1 - core) * 128, 128), 128), :]


def forward(idx, green, gate, probes):
    rows, par_dev = green.shape
    tile = 512
    return pl.pallas_call(
        forward_kernel,
        out_shape=[jax.ShapeDtypeStruct((128, rows), F32)] * 2,
        grid_spec=pltpu.PrefetchScalarGridSpec(
            num_scalar_prefetch=1,
            grid=(rows // tile,),
            in_specs=[
                pl.BlockSpec((tile, par_dev), lambda i, s: (i, 0)),
                pl.BlockSpec((tile // BLK, 1, par_dev), lambda i, s: (i, 0, 0)),
                pl.BlockSpec((par_dev, 256), lambda i, s: (0, 0)),
            ],
            out_specs=[pl.BlockSpec((128, tile), lambda i, s: (0, i))] * 2,
            scratch_shapes=[pltpu.VMEM((256, tile), F32)],
        ),
        compiler_params=vm(30),
        cost_estimate=pl.CostEstimate(
            flops=2 * rows * par_dev * 256, bytes_accessed=rows * par_dev * 2, transcendentals=0
        ),
        name="forward",
    )(idx, green, gate, probes)


def chain_kernel(st_row, st_col, phi, sigma, near, ends, coef):
    row = st_row[0]
    col = st_col[...]
    here = lax.broadcasted_iota(jnp.int32, (CH, CH), 0)
    there = lax.broadcasted_iota(jnp.int32, (CH, CH), 1)
    same = col == row
    prior = jnp.max(jnp.where(same & (here < there), here, -1), axis=0, keepdims=True)
    later = jnp.min(jnp.where(same & (here > there), here, CH), axis=0, keepdims=True)
    near[0] = jnp.where((here == prior) | (here == later), 1.0, 0.0).astype(BF)
    sid = lax.broadcasted_iota(jnp.int32, (128, CH), 0)
    hit = sid == row
    ends[0, :128, :] = jnp.where(hit & (prior < 0), 1.0, 0.0).astype(BF)
    ends[0, 128:, :] = jnp.where(hit & (later >= CH), 1.0, 0.0).astype(BF)
    rate = jnp.sum(jnp.where(hit, phi[...], 0.0), axis=0, keepdims=True)
    level = jnp.sum(jnp.where(hit, sigma[...], 0.0), axis=0, keepdims=True)
    scale = 1.0 / (level * level)
    coef[0:1, :] = (1.0 - rate * rate) * scale
    coef[1:2, :] = rate * rate * scale
    coef[2:3, :] = rate * scale
    coef[3:8, :] = jnp.zeros((5, CH), F32)


def chains(st_all, phi, sigma):
    rows = st_all.shape[0]
    n = rows // CH
    return pl.pallas_call(
        chain_kernel,
        out_shape=[
            jax.ShapeDtypeStruct((n, CH, CH), BF),
            jax.ShapeDtypeStruct((n, 256, CH), BF),
            jax.ShapeDtypeStruct((8, rows), F32),
        ],
        grid=(n,),
        in_specs=[
            pl.BlockSpec((1, 1, CH), lambda i: (i, 0, 0)),
            pl.BlockSpec((CH, 1), lambda i: (i, 0)),
            pl.BlockSpec((128, 1), lambda i: (0, 0)),
            pl.BlockSpec((128, 1), lambda i: (0, 0)),
        ],
        out_specs=[
            pl.BlockSpec((1, CH, CH), lambda i: (i, 0, 0)),
            pl.BlockSpec((1, 256, CH), lambda i: (i, 0, 0)),
            pl.BlockSpec((8, CH), lambda i: (0, i)),
        ],
        compiler_params=vm(16),
        name="chains",
    )(st_all.reshape(n, 1, CH), st_all.reshape(rows, 1), phi.reshape(128, 1), sigma.reshape(128, 1))


def ends_kernel(own, r1, r2, r3, ends, yaug, tips, pay):
    n = ends.shape[0]
    total = own[...] + r1[...].astype(F32) + r2[...].astype(F32) + r3[...].astype(F32)
    yaug[:COLS, :] = total.astype(BF)
    yaug[COLS:, :] = jnp.ones((AUG - COLS, total.shape[1]), BF)
    for b in range(n):
        tips[b] = lax.dot_general(
            yaug[:, b * CH : (b + 1) * CH], ends[b], NT, preferred_element_type=F32
        )
    first = jnp.zeros((AUG, 128), F32)
    last = jnp.zeros((AUG, 128), F32)
    for b in range(n):
        here = tips[b, :, 128:]
        last = jnp.where(here[COLS : COLS + 1, :] > 0.5, here, last)
        here = tips[n - 1 - b, :, :128]
        first = jnp.where(here[COLS : COLS + 1, :] > 0.5, here, first)
    pay[:AUG, :] = first.astype(BF)
    pay[AUG:, :] = last.astype(BF)


def chain_ends(own, recv, ends):
    rows = own.shape[1]
    n = rows // CH
    return pl.pallas_call(
        ends_kernel,
        out_shape=[
            jax.ShapeDtypeStruct((AUG, rows), BF),
            jax.ShapeDtypeStruct((n, AUG, 256), F32),
            jax.ShapeDtypeStruct((2 * AUG, 128), BF),
        ],
        in_specs=[pl.BlockSpec(memory_space=pltpu.VMEM)] * 5,
        out_specs=[pl.BlockSpec(memory_space=pltpu.VMEM)] * 3,
        compiler_params=vm(24),
        name="chain_ends",
    )(own, *recv, ends)


def nearest(me, buf, low, high):
    for j in range(4):
        last = buf[j, AUG:, :].astype(F32)
        ok = jnp.where(me > j, last[COLS : COLS + 1, :], 0.0) > 0.5
        low = jnp.where(ok, last, low)
        first = buf[3 - j, :AUG, :].astype(F32)
        ok = jnp.where(me < 3 - j, first[COLS : COLS + 1, :], 0.0) > 0.5
        high = jnp.where(ok, first, high)
    return low, high


def fill(me, buf, pay, recv):
    buf[me] = pay[...]
    for k, r in enumerate(recv):
        buf[lax.rem(me + 3 - k, 4)] = r[...]


def cross_kernel(idx, pay, r1, r2, r3, low, high, out, buf):
    me = idx[2]
    fill(me, buf, pay, (r1, r2, r3))
    zero = jnp.zeros((AUG, 128), F32)
    a, b = nearest(me, buf, zero, zero)
    low[...] = a
    high[...] = b
    last, _ = nearest(jnp.int32(4), buf, zero, zero)
    _, first = nearest(jnp.int32(-1), buf, zero, zero)
    out[:AUG, :] = first.astype(BF)
    out[AUG:, :] = last.astype(BF)


def cross(idx, pay, recv):
    return pl.pallas_call(
        cross_kernel,
        out_shape=[
            jax.ShapeDtypeStruct((AUG, 128), F32),
            jax.ShapeDtypeStruct((AUG, 128), F32),
            jax.ShapeDtypeStruct((2 * AUG, 128), BF),
        ],
        in_specs=[pl.BlockSpec(memory_space=pltpu.SMEM)] + [pl.BlockSpec(memory_space=pltpu.VMEM)] * 4,
        out_specs=[pl.BlockSpec(memory_space=pltpu.VMEM)] * 3,
        scratch_shapes=[pltpu.VMEM((4, 2 * AUG, 128), BF)],
        compiler_params=vm(8),
        name="cross",
    )(idx, pay, *recv)


def precision_kernel(idx, yaug, tips, near, ends, coef, low, high, pay, r1, r2, r3, out, buf, carry):
    n = near.shape[0]
    me = idx[3]
    fill(me, buf, pay, (r1, r2, r3))
    zero = jnp.zeros((AUG, 128), F32)
    below, above = nearest(me, buf, zero, zero)
    x_below, x_above = low[...], high[...]
    below = jnp.where(x_below[COLS : COLS + 1, :] > 0.5, x_below, below)
    above = jnp.where(x_above[COLS : COLS + 1, :] > 0.5, x_above, above)
    for b in range(n):
        carry[b, :, :128] = below.astype(BF)
        here = tips[b, :, 128:]
        below = jnp.where(here[COLS : COLS + 1, :] > 0.5, here, below)
        e = n - 1 - b
        carry[e, :, 128:] = above.astype(BF)
        here = tips[e, :, :128]
        above = jnp.where(here[COLS : COLS + 1, :] > 0.5, here, above)
    for b in range(n):
        at = slice(b * CH, (b + 1) * CH)
        y = yaug[:, at]
        around = jnp.dot(y, near[b], preferred_element_type=F32) + jnp.dot(
            carry[b], ends[b], preferred_element_type=F32
        )
        alpha = coef[0:1, at] + coef[1:2, at] * around[COLS : COLS + 1, :]
        out[:, at] = (alpha * y[:COLS, :].astype(F32) - coef[2:3, at] * around[:COLS, :]).astype(BF)


def precision(idx, yaug, tips, near, ends, coef, low, high, pay, recv):
    rows = yaug.shape[1]
    n = rows // CH
    return pl.pallas_call(
        precision_kernel,
        out_shape=jax.ShapeDtypeStruct((COLS, rows), BF),
        in_specs=[pl.BlockSpec(memory_space=pltpu.SMEM)] + [pl.BlockSpec(memory_space=pltpu.VMEM)] * 11,
        out_specs=pl.BlockSpec(memory_space=pltpu.VMEM),
        scratch_shapes=[pltpu.VMEM((4, 2 * AUG, 128), BF), pltpu.VMEM((n, AUG, 256), BF)],
        compiler_params=vm(24),
        name="precision",
    )(idx, yaug, tips, near, ends, coef, low, high, pay, *recv)


def adjoint_kernel(axis, idx, *refs):
    pieces, (green, gate) = refs[:8], refs[8:10]
    keep, s1, s2, s3 = refs[10:14]
    panel, acc = refs[14:]
    core, y = idx[0], idx[1]

    @pl.when(pl.program_id(0) == 0)
    def _():
        for k in range(4):
            spot = lax.rem(y + 4 - k, 4) * COLS
            panel[pl.ds(pl.multiple_of(core * 128 + spot, COLS), COLS), :] = pieces[k][...]
            panel[pl.ds(pl.multiple_of((1 - core) * 128 + spot, COLS), COLS), :] = pieces[4 + k][...]

    rows = green.shape[0]
    total = None
    for j in range(rows // 512):
        parts = [
            green[(4 * j + r) * BLK : (4 * j + r + 1) * BLK, :] * gate[4 * j + r].astype(BF)
            for r in range(4)
        ]
        part = jnp.dot(
            panel[:, j * 512 : (j + 1) * 512],
            jnp.concatenate(parts, axis=0),
            preferred_element_type=F32,
        )
        total = part if total is None else total + part
    acc[...] = total
    me = idx[2] if axis == "x" else idx[3]
    for k, ref in enumerate((keep, s1, s2, s3)):
        to = lax.rem(me + k, 4)
        for j in range(4):
            at = j * 64 + to * 16 if axis == "x" else to * 64 + j * 16
            ref[j] = acc[pl.ds(pl.multiple_of(at, 16), 16), :].astype(ref.dtype)


def adjoint(axis, half, idx, pieces, green, gate):
    rows, par_dev = green.shape
    tile = 512
    wide = par_dev // 2
    steps = wide // tile
    shape = (4, 16, wide)
    whole = pl.BlockSpec((COLS, rows), lambda i, s: (0, 0))
    return pl.pallas_call(
        functools.partial(adjoint_kernel, axis),
        out_shape=[jax.ShapeDtypeStruct(shape, F32)] + [jax.ShapeDtypeStruct(shape, BF)] * 3,
        grid_spec=pltpu.PrefetchScalarGridSpec(
            num_scalar_prefetch=1,
            grid=(steps,),
            in_specs=[whole] * 8
            + [
                pl.BlockSpec((rows, tile), lambda i, s: (0, half * steps + i)),
                pl.BlockSpec((rows // BLK, 1, tile), lambda i, s: (0, 0, half * steps + i)),
            ],
            out_specs=[pl.BlockSpec((4, 16, tile), lambda i, s: (0, 0, i))] * 4,
            scratch_shapes=[pltpu.VMEM((256, rows), BF), pltpu.VMEM((256, tile), F32)],
        ),
        compiler_params=vm(40),
        cost_estimate=pl.CostEstimate(
            flops=rows * par_dev * 256, bytes_accessed=rows * par_dev, transcendentals=0
        ),
        name="adjoint_" + axis,
    )(idx, *pieces, green, gate)


def y_shift(v, k):
    return lax.ppermute(v, "par", [(2 * y + c, 2 * ((y + k) % 4) + c) for y in range(4) for c in range(2)])


def core_swap(v):
    return lax.ppermute(v, "par", [(i, i ^ 1) for i in range(8)])


def x_shift(v, k):
    return lax.ppermute(v, "obs", [(4 * z + x, 4 * z + (x + k) % 4) for z in range(4) for x in range(4)])


def z_shift(v, k):
    return lax.ppermute(v, "obs", [(4 * z + x, 4 * ((z + k) % 4) + x) for z in range(4) for x in range(4)])


ORDER = (2, 1, 3)


def spread(shift, parts):
    got = {k: shift(parts[k], k) for k in ORDER}
    return [got[k] for k in (1, 2, 3)]


def pick(v, i):
    return lax.dynamic_index_in_dim(v, i, 0, keepdims=False)


def local(green, blocks, probes, stations, decay, noise_scale):
    par = lax.axis_index("par")
    obs = lax.axis_index("obs")
    core, y = par % 2, par // 2
    x, z = obs % 4, obs // 4
    idx = jnp.stack([core, y, x, z]).astype(jnp.int32)

    st_all = lax.all_gather(stations, "par", axis=0, tiled=True)
    slot = obs * 8 + par
    both = jnp.where(
        jnp.arange(128)[None, :] == slot, jnp.stack([decay, noise_scale]), 0.0
    )
    both = lax.psum(both, ("obs", "par"))
    near, ends, coef = chains(st_all, both[0], both[1])

    gate = jnp.repeat(blocks.astype(F32), BLK, axis=1)[:, None, :]
    mine, send = forward(idx, green, gate, probes)
    total = (mine + core_swap(send)).reshape(4, COLS, -1)
    parts = [pick(total, (y + k) % 4) for k in range(4)]
    recv = spread(y_shift, [None] + [p.astype(BF) for p in parts[1:]])
    yaug, tips, pay = chain_ends(parts[0], recv, ends)

    low, high, pay_z = cross(idx, pay, spread(x_shift, [pay] * 4))
    rows_t = precision(idx, yaug, tips, near, ends, coef, low, high, pay_z, spread(z_shift, [pay_z] * 4))

    pieces = [rows_t] + spread(y_shift, [rows_t] * 4)
    pieces = pieces + [core_swap(p) for p in pieces]

    outs = []
    for half, axis, one, two, where in (
        (0, "x", x_shift, z_shift, z),
        (1, "z", z_shift, x_shift, x),
    ):
        keep, *sends = adjoint(axis, half, idx, pieces, green, gate)
        got = spread(one, [None] + sends)
        mid = keep + got[0].astype(F32) + got[1].astype(F32) + got[2].astype(F32)
        parts = [pick(mid, (where + k) % 4) for k in range(4)]
        got = spread(two, parts)
        outs.append(parts[0] + got[0] + got[1] + got[2])
    return jnp.concatenate(outs, axis=1)


def solution(mesh):
    in_specs = (
        P("obs", "par"),
        P("obs", "par"),
        P("par", None),
        P(("obs", "par")),
        P(("obs", "par")),
        P(("obs", "par")),
    )
    out_specs = P("obs", "par")
    return jax.shard_map(local, mesh=mesh, in_specs=in_specs, out_specs=out_specs, check_vma=False)
```

```python
import functools

import jax
import jax.numpy as jnp
from jax import lax
from jax.experimental import pallas as pl
from jax.experimental.pallas import tpu as pltpu
from jax.sharding import PartitionSpec as P

BLK = 128
CH = 256
AUG = 48
COLS = 32
BF = jnp.bfloat16
F32 = jnp.float32
NT = (((1,), (1,)), ((), ()))
TN = (((0,), (0,)), ((), ()))
MB = 1 << 20
VMEM = pl.BlockSpec(memory_space=pltpu.VMEM)
SMEM = pl.BlockSpec(memory_space=pltpu.SMEM)
HBM = pl.BlockSpec(memory_space=pltpu.HBM)


def shape(dims, dtype):
    return jax.ShapeDtypeStruct(dims, dtype)


def call(kernel, name, out_shape, in_specs, args, scratch=(), mib=16, flops=0, data=0, after=()):
    single = not isinstance(out_shape, list)
    n, m = len(args), len(after)

    def body(*refs):
        kernel(*refs[:n], *refs[n + m :])

    return pl.pallas_call(
        body,
        out_shape=out_shape,
        in_specs=in_specs + [pl.BlockSpec(memory_space=pl.ANY)] * m,
        out_specs=VMEM if single else [VMEM] * len(out_shape),
        scratch_shapes=list(scratch),
        compiler_params=pltpu.CompilerParams(vmem_limit_bytes=mib * MB),
        cost_estimate=pl.CostEstimate(flops=flops, bytes_accessed=data, transcendentals=0),
        name=name,
    )(*args, *after)


def hbm(v):
    return pltpu.with_memory_space_constraint(v, pltpu.HBM)


def fetch(green, start, buf, sem, i):
    tile = buf.shape[0] // sem.shape[0]
    return pltpu.make_async_copy(
        green.at[pl.ds(start + i * tile, tile), :], buf.at[pl.ds(i * tile, tile), :], sem.at[i]
    )


def expand(blocks, gate):
    n, wide = blocks.shape[0], gate.shape[1]
    mine = lax.broadcasted_iota(jnp.int32, (n, wide), 1) // BLK
    pick = jnp.where(mine == lax.broadcasted_iota(jnp.int32, (n, wide), 0), 1.0, 0.0).astype(BF)
    gate[...] = lax.dot_general(
        blocks[...].astype(F32).astype(BF), pick, TN, preferred_element_type=F32
    )


def mask_rows(buf, gate, i, tile, first):
    for r in range(i * tile // BLK, (i + 1) * tile // BLK):
        at = slice(r * BLK, (r + 1) * BLK)
        buf[at, :] = buf[at, :] * gate[first + r : first + r + 1, :].astype(BF)


def forward_kernel(idx, green, blocks, probes, mine, send, buf, own_blocks, own_probes, panel, gate, sem, sem2):
    core = idx[0]
    steps = sem.shape[0]
    tile = buf.shape[0] // steps
    small = [
        pltpu.make_async_copy(blocks, own_blocks, sem2.at[0]),
        pltpu.make_async_copy(probes, own_probes, sem2.at[1]),
    ]
    for copy in small:
        copy.start()
    for i in range(3):
        fetch(green, 0, buf, sem, i).start()
    small[0].wait()
    expand(own_blocks, gate)
    small[1].wait()
    for part in range(2):
        at = pl.multiple_of(lax.rem(part + core, 2) * 128, 128)
        panel[pl.ds(at, 128), :] = own_probes[:, part * 128 : (part + 1) * 128].T
    for i in range(steps):
        fetch(green, 0, buf, sem, i).wait()
        if i + 3 < steps:
            fetch(green, 0, buf, sem, i + 3).start()
        mask_rows(buf, gate, i, tile, 0)
        at = slice(i * tile, (i + 1) * tile)
        part = lax.dot_general(panel[...], buf[at, :], NT, preferred_element_type=F32)
        mine[:, at] = part[:128, :]
        send[:, at] = part[128:, :]


def forward(idx, green, blocks, probes, after=()):
    rows, par_dev = green.shape
    return call(
        forward_kernel,
        "forward",
        [shape((128, rows), F32)] * 2,
        [SMEM, HBM, HBM, HBM],
        (idx, hbm(green), hbm(blocks), hbm(probes)),
        [
            pltpu.VMEM((rows, par_dev), BF),
            pltpu.VMEM(blocks.shape, jnp.int32),
            pltpu.VMEM(probes.shape, BF),
            pltpu.VMEM((256, par_dev), BF),
            pltpu.VMEM((rows // BLK, par_dev), F32),
            pltpu.SemaphoreType.DMA((8,)),
            pltpu.SemaphoreType.DMA((2,)),
        ],
        flops=2 * rows * par_dev * 256,
        data=2 * rows * par_dev,
        mib=32,
        after=after,
    )


def core_sum_kernel(idx, mine, peer, own, s1, s2, s3):
    y = idx[1]
    for k, ref in enumerate((own, s1, s2, s3)):
        at = pl.ds(pl.multiple_of(lax.rem(y + k, 4) * COLS, COLS), COLS)
        ref[...] = (mine[at, :] + peer[at, :]).astype(ref.dtype)


def core_sum(idx, mine, peer, after=()):
    rows = mine.shape[1]
    return call(
        core_sum_kernel,
        "core_sum",
        [shape((COLS, rows), F32)] + [shape((COLS, rows), BF)] * 3,
        [SMEM] + [VMEM] * 2,
        (idx, mine, peer),
        after=after,
    )


def info_kernel(idx, stations, decay, noise_scale, out):
    slot = idx[3] * 32 + idx[2] * 8 + idx[1] * 2 + idx[0]
    lane = lax.broadcasted_iota(jnp.int32, (1, 128), 1)
    rows = [
        stations[...].astype(F32),
        jnp.where(lane == slot, decay[0, 0], 0.0),
        jnp.where(lane == slot, noise_scale[0, 0], 0.0),
        jnp.zeros((2, 128), F32),
    ]
    out[...] = jnp.broadcast_to(jnp.concatenate(rows, axis=0)[None], out.shape)


def info(idx, stations, decay, noise_scale):
    return call(
        info_kernel,
        "info",
        shape((8, 8, 128), F32),
        [SMEM, VMEM, SMEM, SMEM],
        (idx, stations.reshape(4, 128), decay.reshape(1, 1), noise_scale.reshape(1, 1)),
    )


def params_kernel(table, sums):
    sums[...] = jnp.broadcast_to(jnp.sum(table[...], axis=0)[None], sums.shape)


def chain_kernel(table, near, ends, tops, hits):
    held = []
    here = lax.broadcasted_iota(jnp.int32, (CH, CH), 0)
    there = lax.broadcasted_iota(jnp.int32, (CH, CH), 1)
    sid = lax.broadcasted_iota(jnp.int32, (128, CH), 0).astype(F32)
    for b in range(hits.shape[1] // CH):
        at = slice(b * CH, (b + 1) * CH)
        r = (b % 2) * 2
        got = table[b // 2]
        row = jnp.concatenate([got[r : r + 1, :], got[r + 1 : r + 2, :]], axis=1)
        hit = jnp.broadcast_to(row, (128, CH)) == sid
        hit16 = jnp.where(hit, 1.0, 0.0).astype(BF)
        hits[:, at] = hit16
        same = lax.dot_general(hit16, hit16, TN, preferred_element_type=F32) > 0.5
        prior = jnp.max(jnp.where(same & (here < there), here, -1), axis=0, keepdims=True)
        later = jnp.min(jnp.where(same & (here > there), here, CH), axis=0, keepdims=True)
        near[b] = jnp.where((here == prior) | (here == later), 1.0, 0.0).astype(BF)
        ends[:128, at] = jnp.where(hit & (prior < 0), 1.0, 0.0).astype(BF)
        ends[128:, at] = jnp.where(hit & (later >= CH), 1.0, 0.0).astype(BF)
        held.append(jnp.max(jnp.where(hit, 1.0, 0.0), axis=1, keepdims=True))
    n = len(held)
    before = jnp.zeros((128, 1), F32)
    after = jnp.zeros((128, 1), F32)
    for b in range(n):
        at = slice(b * CH, (b + 1) * CH)
        tops[:128, at] = (ends[:128, at].astype(F32) * (1.0 - before)).astype(BF)
        before = jnp.maximum(before, held[b])
        e = n - 1 - b
        at = slice(e * CH, (e + 1) * CH)
        tops[128:, at] = (ends[128:, at].astype(F32) * (1.0 - after)).astype(BF)
        after = jnp.maximum(after, held[e])


def chains(table, rows, after):
    n = rows // CH
    return call(
        chain_kernel,
        "chains",
        [shape((n, CH, CH), BF)] + [shape((256, rows), BF)] * 2 + [shape((128, rows), BF)],
        [VMEM],
        (table,),
        data=12 * MB,
        after=after,
    )


def coef_kernel(params, hits, coef, station):
    total = jnp.sum(params[...], axis=0)
    rate, level = total[4:5, :], total[5:6, :]
    scale = 1.0 / (level * level)
    rows = [(1.0 - rate * rate) * scale, rate * rate * scale, rate * scale]
    for i, row in enumerate(rows):
        station[i : i + 1, :] = row
    station[3:8, :] = jnp.zeros((5, 128), F32)
    split = []
    for row in rows:
        high = row.astype(BF)
        rest = row - high.astype(F32)
        mid = rest.astype(BF)
        split += [high, mid, (rest - mid.astype(F32)).astype(BF)]
    table = jnp.concatenate(split + [jnp.zeros((7, 128), BF)], axis=0)
    out = jnp.dot(table, hits[...], preferred_element_type=F32)
    for i in range(3):
        coef[i : i + 1, :] = out[3 * i : 3 * i + 1, :] + out[3 * i + 1 : 3 * i + 2, :] + out[3 * i + 2 : 3 * i + 3, :]
    coef[3:8, :] = jnp.zeros((5, coef.shape[1]), F32)


def coefs(params, hits):
    return call(
        coef_kernel,
        "coefs",
        [shape((8, hits.shape[1]), F32), shape((8, 128), F32)],
        [VMEM] * 2,
        (params, hits),
    )


def seen(v):
    return v[COLS : COLS + 1, :] > 0.5


def rows_kernel(own_h, r1_h, r2_h, r3_h, near_h, ends_h, coef, out, pay, *scratch):
    own, r1, r2, r3, near, ends, yaug, tips, carry, sem = scratch
    copies = [
        pltpu.make_async_copy(src, dst, sem.at[i])
        for i, (src, dst) in enumerate(
            ((own_h, own), (r1_h, r1), (r2_h, r2), (r3_h, r3), (ends_h, ends), (near_h, near))
        )
    ]
    for copy in copies:
        copy.start()
    for copy in copies[:4]:
        copy.wait()
    n = near.shape[0]
    total = own[...] + r1[...].astype(F32) + r2[...].astype(F32) + r3[...].astype(F32)
    yaug[:COLS, :] = total.astype(BF)
    yaug[COLS:, :] = jnp.ones((AUG - COLS, total.shape[1]), BF)
    copies[4].wait()
    spans = [slice(b * CH, (b + 1) * CH) for b in range(n)]
    for b in range(n):
        tips[b] = lax.dot_general(yaug[:, spans[b]], ends[:, spans[b]], NT, preferred_element_type=F32)
    below = jnp.zeros((AUG, 128), F32)
    above = jnp.zeros((AUG, 128), F32)
    for b in range(n):
        carry[b, :, :128] = below.astype(BF)
        here = tips[b, :, 128:]
        below = jnp.where(seen(here), here, below)
        e = n - 1 - b
        carry[e, :, 128:] = above.astype(BF)
        here = tips[e, :, :128]
        above = jnp.where(seen(here), here, above)
    tip = jnp.concatenate([above, below], axis=0).astype(BF)
    pay[...] = jnp.broadcast_to(tip[None], pay.shape)
    copies[5].wait()
    for b in range(n):
        y = yaug[:, spans[b]]
        around = jnp.dot(y, near[b], preferred_element_type=F32) + jnp.dot(
            carry[b], ends[:, spans[b]], preferred_element_type=F32
        )
        alpha = coef[0:1, spans[b]] + coef[1:2, spans[b]] * around[COLS : COLS + 1, :]
        out[:, spans[b]] = (
            alpha * y[:COLS, :].astype(F32) - coef[2:3, spans[b]] * around[:COLS, :]
        ).astype(BF)


def group_rows(own, recv, near, ends, coef):
    rows = own.shape[1]
    n = rows // CH
    return call(
        rows_kernel,
        "group_rows",
        [shape((COLS, rows), BF), shape((16, 2 * AUG, 128), BF)],
        [HBM] * 6 + [VMEM],
        (*map(hbm, (own, *recv, near, ends)), coef),
        [pltpu.VMEM((COLS, rows), F32)]
        + [pltpu.VMEM((COLS, rows), BF)] * 3
        + [pltpu.VMEM((n, CH, CH), BF), pltpu.VMEM((256, rows), BF)]
        + [pltpu.VMEM((AUG, rows), BF), pltpu.VMEM((n, AUG, 256), F32), pltpu.VMEM((n, AUG, 256), BF)]
        + [pltpu.SemaphoreType.DMA((6,))],
    )


def tie_kernel(idx, station, pay, out):
    me = idx[3] * 4 + idx[2]
    n = pay.shape[0]
    low = jnp.zeros((AUG, 128), F32)
    high = jnp.zeros((AUG, 128), F32)
    for j in range(n - 1):
        last = pay[j, AUG:, :].astype(F32)
        low = jnp.where(jnp.where(me > j, last[COLS : COLS + 1, :], 0.0) > 0.5, last, low)
        e = n - 1 - j
        first = pay[e, :AUG, :].astype(F32)
        high = jnp.where(jnp.where(me < e, first[COLS : COLS + 1, :], 0.0) > 0.5, first, high)
    square, rate = station[1:2, :], station[2:3, :]
    own = pay[me].astype(F32)
    for at, base, other in ((0, own[:AUG, :], low), (128, own[AUG:, :], high)):
        value = square * base[:COLS, :] - rate * other[:COLS, :]
        value = jnp.where(seen(base) & seen(other), value, 0.0).astype(BF)
        out[:, :, at : at + 128] = jnp.broadcast_to(value[None], (8, COLS, 128))


def tie(idx, station, pay, after):
    return call(
        tie_kernel, "tie", shape((8, COLS, 256), BF), [SMEM] + [VMEM] * 2, (idx, station, pay), after=after
    )


def panel_product(green, blocks, copies, panel, buf, own_blocks, acc, gate, sem, sem_blocks):
    steps = sem.shape[0]
    tile = buf.shape[0] // steps
    small = pltpu.make_async_copy(blocks, own_blocks, sem_blocks)
    small.start()
    for copy in copies:
        copy.start()
    for i in range(3):
        fetch(green, 0, buf, sem, i).start()
    small.wait()
    expand(own_blocks, gate)
    for copy in copies:
        copy.wait()
    for i in range(steps):
        fetch(green, 0, buf, sem, i).wait()
        if i + 3 < steps:
            fetch(green, 0, buf, sem, i + 3).start()
        mask_rows(buf, gate, i, tile, 0)
        at = slice(i * tile, (i + 1) * tile)
        part = jnp.dot(panel[:, at], buf[at, :], preferred_element_type=F32)
        acc[...] = part if i == 0 else acc[...] + part


def product_scratch(rows, par_dev, blocks):
    return [
        pltpu.VMEM((256, rows), BF),
        pltpu.VMEM((rows, par_dev), BF),
        pltpu.VMEM(blocks.shape, jnp.int32),
        pltpu.VMEM((256, par_dev), F32),
        pltpu.VMEM((rows // BLK, par_dev), F32),
        pltpu.SemaphoreType.DMA((8,)),
        pltpu.SemaphoreType.DMA((9,)),
    ]


def end_rows_kernel(green, blocks, tops, out, panel, buf, own_blocks, acc, gate, sem, sem2):
    copies = [pltpu.make_async_copy(tops, panel, sem2.at[0])]
    panel_product(green, blocks, copies, panel, buf, own_blocks, acc, gate, sem, sem2.at[8])
    out[...] = acc[...].astype(BF)


def end_rows(green, blocks, tops, after):
    rows, par_dev = green.shape
    return call(
        end_rows_kernel,
        "end_rows",
        shape((256, par_dev), BF),
        [HBM] * 3,
        tuple(map(hbm, (green, blocks, tops))),
        product_scratch(rows, par_dev, blocks),
        flops=2 * rows * par_dev * 256,
        data=2 * rows * par_dev,
        mib=32,
        after=after,
    )


def adjoint_kernel(idx, *refs):
    pieces, (green, blocks, out) = refs[:8], refs[8:11]
    panel, buf, own_blocks, acc, gate, sem, sem2 = refs[11:]
    core, y = idx[0], idx[1]
    copies = []
    for k in range(4):
        spot = lax.rem(y + 4 - k, 4) * COLS
        for base, j in ((core, k), (1 - core, 4 + k)):
            at = pl.ds(pl.multiple_of(base * 128 + spot, COLS), COLS)
            copies.append(pltpu.make_async_copy(pieces[j], panel.at[at, :], sem2.at[j]))
    panel_product(green, blocks, copies, panel, buf, own_blocks, acc, gate, sem, sem2.at[8])
    out[...] = acc[...]


def adjoint(idx, pieces, green, blocks, after=()):
    rows, par_dev = green.shape
    return call(
        adjoint_kernel,
        "adjoint",
        shape((256, par_dev), F32),
        [SMEM] + [HBM] * 10,
        (idx, *map(hbm, (*pieces, green, blocks))),
        product_scratch(rows, par_dev, blocks),
        flops=2 * rows * par_dev * 256,
        data=2 * rows * par_dev,
        mib=32,
        after=after,
    )


def finish_kernel(axis, idx, product, tied, rows_g, keep, s1, s2, s3, ties, acc):
    for p in range(8):
        at = (p % 2) * 128 + (p // 2) * COLS
        ties[at : at + COLS, :] = tied[p]
    wide = acc.shape[1]
    at = slice(0, wide) if axis == "x" else slice(wide, 2 * wide)
    acc[...] = product[:, at] + jnp.dot(ties[...], rows_g[:, at], preferred_element_type=F32)
    me = idx[2] if axis == "x" else idx[3]
    for k, ref in enumerate((keep, s1, s2, s3)):
        to = lax.rem(me + k, 4)
        for j in range(4):
            row = j * 64 + to * 16 if axis == "x" else to * 64 + j * 16
            ref[j] = acc[pl.ds(pl.multiple_of(row, 16), 16), :].astype(ref.dtype)


def finish(axis, idx, product, tied, rows_g, after=()):
    wide = product.shape[1] // 2
    return call(
        functools.partial(finish_kernel, axis),
        "finish_" + axis,
        [shape((4, 16, wide), F32)] + [shape((4, 16, wide), BF)] * 3,
        [SMEM] + [VMEM] * 3,
        (idx, product, tied, rows_g),
        [pltpu.VMEM((256, 256), BF), pltpu.VMEM((256, wide), F32)],
        after=after,
    )


def fold_kernel(which, idx, keep, r1, r2, r3, own, s1, s2, s3):
    me = idx[which]
    for k, ref in enumerate((own, s1, s2, s3)):
        to = lax.rem(me + k, 4)
        ref[...] = keep[to] + r1[to].astype(F32) + r2[to].astype(F32) + r3[to].astype(F32)


def fold(which, idx, keep, recv):
    wide = keep.shape[2]
    return call(
        functools.partial(fold_kernel, which),
        "fold",
        [shape((16, wide), F32)] * 4,
        [SMEM] + [VMEM] * 4,
        (idx, keep, *recv),
    )


def y_shift(v, k):
    return lax.ppermute(v, "par", [(2 * y + c, 2 * ((y + k) % 4) + c) for y in range(4) for c in range(2)])


def core_swap(v):
    return lax.ppermute(v, "par", [(i, i ^ 1) for i in range(8)])


def x_shift(v, k):
    return lax.ppermute(v, "obs", [(4 * z + x, 4 * z + (x + k) % 4) for z in range(4) for x in range(4)])


def z_shift(v, k):
    return lax.ppermute(v, "obs", [(4 * z + x, 4 * ((z + k) % 4) + x) for z in range(4) for x in range(4)])


def exchange(v, axes):
    return lax.all_to_all(v, axes, split_axis=0, concat_axis=0, tiled=True)


def spread(shift, parts):
    got = {k: shift(parts[k - 1], k) for k in (2, 1, 3)}
    return [got[k] for k in (1, 2, 3)]


def local(green, blocks, probes, stations, decay, noise_scale):
    par = lax.axis_index("par")
    obs = lax.axis_index("obs")
    idx = jnp.stack([par % 2, par // 2, obs % 4, obs // 4]).astype(jnp.int32)
    blocks = blocks.T

    mail = info(idx, stations, decay, noise_scale)
    stations_g = exchange(mail, "par")
    mine, send = forward(idx, green, blocks, probes, after=(mail,))
    params = call(params_kernel, "params", shape((16, 8, 128), F32), [VMEM], (stations_g,), after=(send,))

    own, *sends = core_sum(idx, mine, core_swap(send), after=(params,))
    recv = spread(y_shift, sends)
    near, ends, tops, hits = chains(stations_g, green.shape[0], after=(own,))
    coef, station = coefs(exchange(params, "obs"), hits)

    rows_t, pay = group_rows(own, recv, near, ends, coef)
    pieces = [rows_t] + spread(y_shift, [rows_t] * 3)
    pay = exchange(pay, "obs")
    rows_g = end_rows(green, blocks, tops, after=(rows_t,))
    tied = tie(idx, station, pay, after=(rows_g,))
    pieces = pieces + [core_swap(p) for p in pieces]
    product = adjoint(idx, pieces, green, blocks, after=(tied,))
    tied = exchange(tied, "par")
    half0 = finish("x", idx, product, tied, rows_g)
    half1 = finish("z", idx, product, tied, rows_g, after=(half0[1],))

    outs = []
    for (keep, *sends), one, two, which in ((half0, x_shift, z_shift, 3), (half1, z_shift, x_shift, 2)):
        last, *sends = fold(which, idx, keep, spread(one, sends))
        got = spread(two, sends)
        outs.append(last + got[0] + got[1] + got[2])
    return jnp.concatenate(outs, axis=1)


def solution(mesh):
    in_specs = (
        P("obs", "par"),
        P("obs", "par"),
        P("par", None),
        P(("obs", "par")),
        P(("obs", "par")),
        P(("obs", "par")),
    )
    out_specs = P("obs", "par")
    return jax.shard_map(local, mesh=mesh, in_specs=in_specs, out_specs=out_specs, check_vma=False)
```

```python
import functools

import jax
import jax.numpy as jnp
from jax import lax
from jax.experimental import pallas as pl
from jax.experimental.pallas import tpu as pltpu
from jax.sharding import PartitionSpec as P

BLK = 128
CH = 256
AUG = 48
COLS = 32
BF = jnp.bfloat16
F32 = jnp.float32
NT = (((1,), (1,)), ((), ()))
TN = (((0,), (0,)), ((), ()))
MB = 1 << 20
VMEM = pl.BlockSpec(memory_space=pltpu.VMEM)
SMEM = pl.BlockSpec(memory_space=pltpu.SMEM)
HBM = pl.BlockSpec(memory_space=pltpu.HBM)


def shape(dims, dtype):
    return jax.ShapeDtypeStruct(dims, dtype)


def call(kernel, name, out_shape, in_specs, args, scratch=(), mib=16, flops=0, data=0, after=(), out_specs=None):
    single = not isinstance(out_shape, list)
    n, m = len(args), len(after)

    def body(*refs):
        kernel(*refs[:n], *refs[n + m :])

    return pl.pallas_call(
        body,
        out_shape=out_shape,
        in_specs=in_specs + [pl.BlockSpec(memory_space=pl.ANY)] * m,
        out_specs=out_specs or (VMEM if single else [VMEM] * len(out_shape)),
        scratch_shapes=list(scratch),
        compiler_params=pltpu.CompilerParams(vmem_limit_bytes=mib * MB),
        cost_estimate=pl.CostEstimate(flops=flops, bytes_accessed=data, transcendentals=0),
        name=name,
    )(*args, *after)


def hbm(v):
    return pltpu.with_memory_space_constraint(v, pltpu.HBM)


def fetch(green, start, buf, sem, i):
    tile = buf.shape[0] // sem.shape[0]
    return pltpu.make_async_copy(
        green.at[pl.ds(start + i * tile, tile), :], buf.at[pl.ds(i * tile, tile), :], sem.at[i]
    )


def expand(blocks, gate):
    n, wide = blocks.shape[0], gate.shape[1]
    mine = lax.broadcasted_iota(jnp.int32, (n, wide), 1) // BLK
    pick = jnp.where(mine == lax.broadcasted_iota(jnp.int32, (n, wide), 0), 1.0, 0.0).astype(BF)
    gate[...] = lax.dot_general(
        blocks[...].astype(F32).astype(BF), pick, TN, preferred_element_type=F32
    )


def mask_rows(buf, gate, i, tile, first):
    for r in range(i * tile // BLK, (i + 1) * tile // BLK):
        at = slice(r * BLK, (r + 1) * BLK)
        buf[at, :] = buf[at, :] * gate[first + r : first + r + 1, :].astype(BF)


def forward_kernel(idx, green, blocks, probes, mine, send, buf, own_blocks, own_probes, panel, gate, sem, sem2):
    core = idx[0]
    steps = sem.shape[0]
    tile = buf.shape[0] // steps
    small = [
        pltpu.make_async_copy(blocks, own_blocks, sem2.at[0]),
        pltpu.make_async_copy(probes, own_probes, sem2.at[1]),
    ]
    for copy in small:
        copy.start()
    for i in range(2):
        fetch(green, 0, buf, sem, i).start()
    small[0].wait()
    expand(own_blocks, gate)
    small[1].wait()
    for part in range(2):
        at = pl.multiple_of(lax.rem(part + core, 2) * 128, 128)
        panel[pl.ds(at, 128), :] = own_probes[:, part * 128 : (part + 1) * 128].T
    for i in range(steps):
        fetch(green, 0, buf, sem, i).wait()
        if i + 2 < steps:
            fetch(green, 0, buf, sem, i + 2).start()
        mask_rows(buf, gate, i, tile, 0)
        at = slice(i * tile, (i + 1) * tile)
        part = lax.dot_general(panel[...], buf[at, :], NT, preferred_element_type=F32)
        mine[:, at] = part[:128, :]
        send[:, at] = part[128:, :]


def forward(idx, green, blocks, probes, after=()):
    rows, par_dev = green.shape
    return call(
        forward_kernel,
        "forward",
        [shape((128, rows), F32)] * 2,
        [SMEM, HBM, HBM, HBM],
        (idx, hbm(green), hbm(blocks), hbm(probes)),
        [
            pltpu.VMEM((rows, par_dev), BF),
            pltpu.VMEM(blocks.shape, jnp.int32),
            pltpu.VMEM(probes.shape, BF),
            pltpu.VMEM((256, par_dev), BF),
            pltpu.VMEM((rows // BLK, par_dev), F32),
            pltpu.SemaphoreType.DMA((8,)),
            pltpu.SemaphoreType.DMA((2,)),
        ],
        flops=2 * rows * par_dev * 256,
        data=2 * rows * par_dev,
        mib=32,
        after=after,
    )


def core_sum_kernel(idx, mine, peer, own, s1, s2, s3):
    y = idx[1]
    for k, ref in enumerate((own, s1, s2, s3)):
        at = pl.ds(pl.multiple_of(lax.rem(y + k, 4) * COLS, COLS), COLS)
        ref[...] = (mine[at, :] + peer[at, :]).astype(ref.dtype)


def core_sum(idx, mine, peer, after=()):
    rows = mine.shape[1]
    return call(
        core_sum_kernel,
        "core_sum",
        [shape((COLS, rows), F32)] + [shape((COLS, rows), BF)] * 3,
        [SMEM] + [VMEM] * 2,
        (idx, mine, peer),
        after=after,
    )


def info_kernel(idx, stations, decay, noise_scale, out):
    slot = idx[3] * 32 + idx[2] * 8 + idx[1] * 2 + idx[0]
    lane = lax.broadcasted_iota(jnp.int32, (1, 128), 1)
    rows = [
        stations[...].astype(F32),
        jnp.where(lane == slot, decay[0, 0], 0.0),
        jnp.where(lane == slot, noise_scale[0, 0], 0.0),
        jnp.zeros((2, 128), F32),
    ]
    out[...] = jnp.broadcast_to(jnp.concatenate(rows, axis=0)[None], out.shape)


def info(idx, stations, decay, noise_scale):
    return call(
        info_kernel,
        "info",
        shape((8, 8, 128), F32),
        [SMEM, VMEM, SMEM, SMEM],
        (idx, stations.reshape(4, 128), decay.reshape(1, 1), noise_scale.reshape(1, 1)),
    )


def params_kernel(table, sums):
    sums[...] = jnp.broadcast_to(jnp.sum(table[...], axis=0)[None], sums.shape)


def chain_kernel(table, near_h, ends_h, tops_h, hits, near, ends, tops, sem):
    held = []
    copies = []

    def send(src, dst, i):
        copies.append(pltpu.make_async_copy(src, dst, sem.at[i]))
        copies[-1].start()

    here = lax.broadcasted_iota(jnp.int32, (CH, CH), 0)
    there = lax.broadcasted_iota(jnp.int32, (CH, CH), 1)
    sid = lax.broadcasted_iota(jnp.int32, (128, CH), 0).astype(F32)
    n = hits.shape[1] // CH
    for b in range(n):
        at = slice(b * CH, (b + 1) * CH)
        r = (b % 2) * 2
        got = table[b // 2]
        row = jnp.concatenate([got[r : r + 1, :], got[r + 1 : r + 2, :]], axis=1)
        hit = jnp.broadcast_to(row, (128, CH)) == sid
        hit16 = jnp.where(hit, 1.0, 0.0).astype(BF)
        hits[:, at] = hit16
        same = lax.dot_general(hit16, hit16, TN, preferred_element_type=F32) > 0.5
        prior = jnp.max(jnp.where(same & (here < there), here, -1), axis=0, keepdims=True)
        later = jnp.min(jnp.where(same & (here > there), here, CH), axis=0, keepdims=True)
        near[b] = jnp.where((here == prior) | (here == later), 1.0, 0.0).astype(BF)
        ends[:128, at] = jnp.where(hit & (prior < 0), 1.0, 0.0).astype(BF)
        ends[128:, at] = jnp.where(hit & (later >= CH), 1.0, 0.0).astype(BF)
        held.append(jnp.max(jnp.where(hit, 1.0, 0.0), axis=1, keepdims=True))
        if b == n // 2 - 1:
            send(near.at[pl.ds(0, n // 2)], near_h.at[pl.ds(0, n // 2)], 0)
    send(near.at[pl.ds(n // 2, n // 2)], near_h.at[pl.ds(n // 2, n // 2)], 1)
    send(ends, ends_h, 2)
    before = jnp.zeros((128, 1), F32)
    after = jnp.zeros((128, 1), F32)
    for b in range(n):
        at = slice(b * CH, (b + 1) * CH)
        tops[:128, at] = (ends[:128, at].astype(F32) * (1.0 - before)).astype(BF)
        before = jnp.maximum(before, held[b])
        e = n - 1 - b
        at = slice(e * CH, (e + 1) * CH)
        tops[128:, at] = (ends[128:, at].astype(F32) * (1.0 - after)).astype(BF)
        after = jnp.maximum(after, held[e])
    send(tops, tops_h, 3)
    for copy in copies:
        copy.wait()


def chains(table, rows, after):
    n = rows // CH
    return call(
        chain_kernel,
        "chains",
        [pltpu.HBM((n, CH, CH), BF)] + [pltpu.HBM((256, rows), BF)] * 2 + [shape((128, rows), BF)],
        [VMEM],
        (table,),
        [pltpu.VMEM((n, CH, CH), BF)] + [pltpu.VMEM((256, rows), BF)] * 2 + [pltpu.SemaphoreType.DMA((4,))],
        data=12 * MB,
        after=after,
        out_specs=[HBM] * 3 + [VMEM],
    )


def coef_kernel(params, hits, coef, station):
    total = jnp.sum(params[...], axis=0)
    rate, level = total[4:5, :], total[5:6, :]
    scale = 1.0 / (level * level)
    rows = [(1.0 - rate * rate) * scale, rate * rate * scale, rate * scale]
    for i, row in enumerate(rows):
        station[i : i + 1, :] = row
    station[3:8, :] = jnp.zeros((5, 128), F32)
    split = []
    for row in rows:
        high = row.astype(BF)
        rest = row - high.astype(F32)
        mid = rest.astype(BF)
        split += [high, mid, (rest - mid.astype(F32)).astype(BF)]
    table = jnp.concatenate(split + [jnp.zeros((7, 128), BF)], axis=0)
    out = jnp.dot(table, hits[...], preferred_element_type=F32)
    for i in range(3):
        coef[i : i + 1, :] = out[3 * i : 3 * i + 1, :] + out[3 * i + 1 : 3 * i + 2, :] + out[3 * i + 2 : 3 * i + 3, :]
    coef[3:8, :] = jnp.zeros((5, coef.shape[1]), F32)


def coefs(params, hits):
    return call(
        coef_kernel,
        "coefs",
        [shape((8, hits.shape[1]), F32), shape((8, 128), F32)],
        [VMEM] * 2,
        (params, hits),
    )


def seen(v):
    return v[COLS : COLS + 1, :] > 0.5


def rows_kernel(own_h, r1_h, r2_h, r3_h, near_h, ends_h, coef, out, pay, *scratch):
    own, r1, r2, r3, near, ends, yaug, tips, carry, sem = scratch
    copies = [
        pltpu.make_async_copy(src, dst, sem.at[i])
        for i, (src, dst) in enumerate(
            ((own_h, own), (r1_h, r1), (r2_h, r2), (r3_h, r3), (ends_h, ends), (near_h, near))
        )
    ]
    for copy in copies:
        copy.start()
    for copy in copies[:4]:
        copy.wait()
    n = near.shape[0]
    total = own[...] + r1[...].astype(F32) + r2[...].astype(F32) + r3[...].astype(F32)
    yaug[:COLS, :] = total.astype(BF)
    yaug[COLS:, :] = jnp.ones((AUG - COLS, total.shape[1]), BF)
    copies[4].wait()
    spans = [slice(b * CH, (b + 1) * CH) for b in range(n)]
    for b in range(n):
        tips[b] = lax.dot_general(yaug[:, spans[b]], ends[:, spans[b]], NT, preferred_element_type=F32)
    below = jnp.zeros((AUG, 128), F32)
    above = jnp.zeros((AUG, 128), F32)
    for b in range(n):
        carry[b, :, :128] = below.astype(BF)
        here = tips[b, :, 128:]
        below = jnp.where(seen(here), here, below)
        e = n - 1 - b
        carry[e, :, 128:] = above.astype(BF)
        here = tips[e, :, :128]
        above = jnp.where(seen(here), here, above)
    tip = jnp.concatenate([above, below], axis=0).astype(BF)
    pay[...] = jnp.broadcast_to(tip[None], pay.shape)
    copies[5].wait()
    for b in range(n):
        y = yaug[:, spans[b]]
        around = jnp.dot(y, near[b], preferred_element_type=F32) + jnp.dot(
            carry[b], ends[:, spans[b]], preferred_element_type=F32
        )
        alpha = coef[0:1, spans[b]] + coef[1:2, spans[b]] * around[COLS : COLS + 1, :]
        out[:, spans[b]] = (
            alpha * y[:COLS, :].astype(F32) - coef[2:3, spans[b]] * around[:COLS, :]
        ).astype(BF)


def group_rows(own, recv, near, ends, coef):
    rows = own.shape[1]
    n = rows // CH
    return call(
        rows_kernel,
        "group_rows",
        [shape((COLS, rows), BF), shape((16, 2 * AUG, 128), BF)],
        [HBM] * 6 + [VMEM],
        (*map(hbm, (own, *recv, near, ends)), coef),
        [pltpu.VMEM((COLS, rows), F32)]
        + [pltpu.VMEM((COLS, rows), BF)] * 3
        + [pltpu.VMEM((n, CH, CH), BF), pltpu.VMEM((256, rows), BF)]
        + [pltpu.VMEM((AUG, rows), BF), pltpu.VMEM((n, AUG, 256), F32), pltpu.VMEM((n, AUG, 256), BF)]
        + [pltpu.SemaphoreType.DMA((6,))],
    )


def tie_kernel(idx, station, pay, out):
    me = idx[3] * 4 + idx[2]
    n = pay.shape[0]
    low = jnp.zeros((AUG, 128), F32)
    high = jnp.zeros((AUG, 128), F32)
    for j in range(n - 1):
        last = pay[j, AUG:, :].astype(F32)
        low = jnp.where(jnp.where(me > j, last[COLS : COLS + 1, :], 0.0) > 0.5, last, low)
        e = n - 1 - j
        first = pay[e, :AUG, :].astype(F32)
        high = jnp.where(jnp.where(me < e, first[COLS : COLS + 1, :], 0.0) > 0.5, first, high)
    square, rate = station[1:2, :], station[2:3, :]
    own = pay[me].astype(F32)
    for at, base, other in ((0, own[:AUG, :], low), (128, own[AUG:, :], high)):
        value = square * base[:COLS, :] - rate * other[:COLS, :]
        value = jnp.where(seen(base) & seen(other), value, 0.0).astype(BF)
        out[:, :, at : at + 128] = jnp.broadcast_to(value[None], (8, COLS, 128))


def tie(idx, station, pay, after):
    return call(
        tie_kernel, "tie", shape((8, COLS, 256), BF), [SMEM] + [VMEM] * 2, (idx, station, pay), after=after
    )


def panel_product(green, blocks, copies, panel, buf, own_blocks, acc, gate, sem, sem_blocks):
    steps = sem.shape[0]
    tile = buf.shape[0] // steps
    small = pltpu.make_async_copy(blocks, own_blocks, sem_blocks)
    small.start()
    for copy in copies:
        copy.start()
    for i in range(3):
        fetch(green, 0, buf, sem, i).start()
    small.wait()
    expand(own_blocks, gate)
    for copy in copies:
        copy.wait()
    for i in range(steps):
        fetch(green, 0, buf, sem, i).wait()
        if i + 3 < steps:
            fetch(green, 0, buf, sem, i + 3).start()
        mask_rows(buf, gate, i, tile, 0)
        at = slice(i * tile, (i + 1) * tile)
        part = jnp.dot(panel[:, at], buf[at, :], preferred_element_type=F32)
        acc[...] = part if i == 0 else acc[...] + part


def product_scratch(rows, par_dev, blocks):
    return [
        pltpu.VMEM((256, rows), BF),
        pltpu.VMEM((rows, par_dev), BF),
        pltpu.VMEM(blocks.shape, jnp.int32),
        pltpu.VMEM((256, par_dev), F32),
        pltpu.VMEM((rows // BLK, par_dev), F32),
        pltpu.SemaphoreType.DMA((8,)),
        pltpu.SemaphoreType.DMA((9,)),
    ]


def end_rows_kernel(green, blocks, tops, out, panel, buf, own_blocks, acc, gate, sem, sem2):
    copies = [pltpu.make_async_copy(tops, panel, sem2.at[0])]
    panel_product(green, blocks, copies, panel, buf, own_blocks, acc, gate, sem, sem2.at[8])
    out[...] = acc[...].astype(BF)


def end_rows(green, blocks, tops, after):
    rows, par_dev = green.shape
    return call(
        end_rows_kernel,
        "end_rows",
        shape((256, par_dev), BF),
        [HBM] * 3,
        tuple(map(hbm, (green, blocks, tops))),
        product_scratch(rows, par_dev, blocks),
        flops=2 * rows * par_dev * 256,
        data=2 * rows * par_dev,
        mib=32,
        after=after,
    )


def adjoint_kernel(idx, *refs):
    pieces, (green, blocks, out) = refs[:8], refs[8:11]
    panel, buf, own_blocks, acc, gate, sem, sem2 = refs[11:]
    core, y = idx[0], idx[1]
    copies = []
    for k in range(4):
        spot = lax.rem(y + 4 - k, 4) * COLS
        for base, j in ((core, k), (1 - core, 4 + k)):
            at = pl.ds(pl.multiple_of(base * 128 + spot, COLS), COLS)
            copies.append(pltpu.make_async_copy(pieces[j], panel.at[at, :], sem2.at[j]))
    panel_product(green, blocks, copies, panel, buf, own_blocks, acc, gate, sem, sem2.at[8])
    out[...] = acc[...]


def adjoint(idx, pieces, green, blocks, after=()):
    rows, par_dev = green.shape
    return call(
        adjoint_kernel,
        "adjoint",
        shape((256, par_dev), F32),
        [SMEM] + [HBM] * 10,
        (idx, *map(hbm, (*pieces, green, blocks))),
        product_scratch(rows, par_dev, blocks),
        flops=2 * rows * par_dev * 256,
        data=2 * rows * par_dev,
        mib=32,
        after=after,
    )


def finish_kernel(product, tied, rows_g, out, ties):
    for p in range(8):
        at = (p % 2) * 128 + (p // 2) * COLS
        ties[at : at + COLS, :] = tied[p]
    tile = 512
    for c in range(0, product.shape[1], tile):
        at = slice(c, c + tile)
        total = product[:, at] + jnp.dot(ties[...], rows_g[:, at], preferred_element_type=F32)
        out[:, :, at] = total.reshape(16, 16, tile).astype(BF)


def total_kernel(parts, out):
    total = parts[0].astype(F32)
    for j in range(1, parts.shape[0]):
        total = total + parts[j].astype(F32)
    out[...] = total


def y_shift(v, k):
    return lax.ppermute(v, "par", [(2 * y + c, 2 * ((y + k) % 4) + c) for y in range(4) for c in range(2)])


def core_swap(v):
    return lax.ppermute(v, "par", [(i, i ^ 1) for i in range(8)])


def x_shift(v, k):
    return lax.ppermute(v, "obs", [(4 * z + x, 4 * z + (x + k) % 4) for z in range(4) for x in range(4)])


def z_shift(v, k):
    return lax.ppermute(v, "obs", [(4 * z + x, 4 * ((z + k) % 4) + x) for z in range(4) for x in range(4)])


def exchange(v, axes):
    return lax.all_to_all(v, axes, split_axis=0, concat_axis=0, tiled=True)


def spread(shift, parts):
    got = {k: shift(parts[k - 1], k) for k in (2, 1, 3)}
    return [got[k] for k in (1, 2, 3)]


def local(green, blocks, probes, stations, decay, noise_scale):
    par = lax.axis_index("par")
    obs = lax.axis_index("obs")
    idx = jnp.stack([par % 2, par // 2, obs % 4, obs // 4]).astype(jnp.int32)
    blocks = blocks.T

    mail = info(idx, stations, decay, noise_scale)
    stations_g = exchange(mail, "par")
    mine, send = forward(idx, green, blocks, probes, after=(mail,))
    params = call(params_kernel, "params", shape((16, 8, 128), F32), [VMEM], (stations_g,), after=(send,))

    own, *sends = core_sum(idx, mine, core_swap(send), after=(params,))
    recv = spread(y_shift, sends)
    near, ends, tops, hits = chains(stations_g, green.shape[0], after=(own,))
    coef, station = coefs(exchange(params, "obs"), hits)

    rows_t, pay = group_rows(own, recv, near, ends, coef)
    pieces = [rows_t] + spread(y_shift, [rows_t] * 3)
    pay = exchange(pay, "obs")
    rows_g = end_rows(green, blocks, tops, after=(rows_t,))
    tied = tie(idx, station, pay, after=(rows_g,))
    pieces = pieces + [core_swap(p) for p in pieces]
    product = adjoint(idx, pieces, green, blocks, after=(tied,))
    tied = exchange(tied, "par")
    wide = green.shape[1]
    parts = call(
        finish_kernel,
        "finish",
        shape((16, 16, wide), BF),
        [VMEM] * 3,
        (product, tied, rows_g),
        [pltpu.VMEM((256, 256), BF)],
    )
    return call(total_kernel, "total", shape((16, wide), F32), [VMEM], (exchange(parts, "obs"),))


def solution(mesh):
    in_specs = (
        P("obs", "par"),
        P("obs", "par"),
        P("par", None),
        P(("obs", "par")),
        P(("obs", "par")),
        P(("obs", "par")),
    )
    out_specs = P("obs", "par")
    return jax.shard_map(local, mesh=mesh, in_specs=in_specs, out_specs=out_specs, check_vma=False)
```

```python
import functools

import jax
import jax.numpy as jnp
from jax import lax
from jax.experimental import pallas as pl
from jax.experimental.pallas import tpu as pltpu
from jax.sharding import PartitionSpec as P

BLK = 128
CH = 256
AUG = 48
COLS = 32
BF = jnp.bfloat16
F32 = jnp.float32
NT = (((1,), (1,)), ((), ()))
TN = (((0,), (0,)), ((), ()))
MB = 1 << 20
VMEM = pl.BlockSpec(memory_space=pltpu.VMEM)
SMEM = pl.BlockSpec(memory_space=pltpu.SMEM)
HBM = pl.BlockSpec(memory_space=pltpu.HBM)


def shape(dims, dtype):
    return jax.ShapeDtypeStruct(dims, dtype)


def call(kernel, name, out_shape, in_specs, args, scratch=(), mib=16, flops=0, data=0, after=(), out_specs=None):
    single = not isinstance(out_shape, list)
    n, m = len(args), len(after)

    def body(*refs):
        kernel(*refs[:n], *refs[n + m :])

    return pl.pallas_call(
        body,
        out_shape=out_shape,
        in_specs=in_specs + [pl.BlockSpec(memory_space=pl.ANY)] * m,
        out_specs=out_specs or (VMEM if single else [VMEM] * len(out_shape)),
        scratch_shapes=list(scratch),
        compiler_params=pltpu.CompilerParams(vmem_limit_bytes=mib * MB),
        cost_estimate=pl.CostEstimate(flops=flops, bytes_accessed=data, transcendentals=0),
        name=name,
    )(*args, *after)


def hbm(v):
    return pltpu.with_memory_space_constraint(v, pltpu.HBM)


def fetch(green, start, buf, sem, i):
    tile = buf.shape[0] // sem.shape[0]
    return pltpu.make_async_copy(
        green.at[pl.ds(start + i * tile, tile), :], buf.at[pl.ds(i * tile, tile), :], sem.at[i]
    )


def expand(blocks, gate):
    n, wide = blocks.shape[0], gate.shape[1]
    mine = lax.broadcasted_iota(jnp.int32, (n, wide), 1) // BLK
    pick = jnp.where(mine == lax.broadcasted_iota(jnp.int32, (n, wide), 0), 1.0, 0.0).astype(BF)
    gate[...] = lax.dot_general(
        blocks[...].astype(F32).astype(BF), pick, TN, preferred_element_type=F32
    )


def mask_rows(buf, gate, i, tile, first):
    for r in range(i * tile // BLK, (i + 1) * tile // BLK):
        at = slice(r * BLK, (r + 1) * BLK)
        buf[at, :] = buf[at, :] * gate[first + r : first + r + 1, :].astype(BF)


def forward_kernel(idx, green, blocks, probes, mine, send, buf, own_blocks, own_probes, panel, gate, sem, sem2):
    core = idx[0]
    steps = sem.shape[0]
    tile = buf.shape[0] // steps
    small = [
        pltpu.make_async_copy(blocks, own_blocks, sem2.at[0]),
        pltpu.make_async_copy(probes, own_probes, sem2.at[1]),
    ]
    for copy in small:
        copy.start()
    for i in range(3):
        fetch(green, 0, buf, sem, i).start()
    small[0].wait()
    expand(own_blocks, gate)
    small[1].wait()
    for part in range(2):
        at = pl.multiple_of(lax.rem(part + core, 2) * 128, 128)
        panel[pl.ds(at, 128), :] = own_probes[:, part * 128 : (part + 1) * 128].T
    for i in range(steps):
        fetch(green, 0, buf, sem, i).wait()
        if i + 3 < steps:
            fetch(green, 0, buf, sem, i + 3).start()
        mask_rows(buf, gate, i, tile, 0)
        at = slice(i * tile, (i + 1) * tile)
        part = lax.dot_general(panel[...], buf[at, :], NT, preferred_element_type=F32)
        mine[:, at] = part[:128, :]
        send[:, at] = part[128:, :]


def forward(idx, green, blocks, probes, after=()):
    rows, par_dev = green.shape
    return call(
        forward_kernel,
        "forward",
        [shape((128, rows), F32)] * 2,
        [SMEM, HBM, HBM, HBM],
        (idx, hbm(green), hbm(blocks), hbm(probes)),
        [
            pltpu.VMEM((rows, par_dev), BF),
            pltpu.VMEM(blocks.shape, jnp.int32),
            pltpu.VMEM(probes.shape, BF),
            pltpu.VMEM((256, par_dev), BF),
            pltpu.VMEM((rows // BLK, par_dev), F32),
            pltpu.SemaphoreType.DMA((16,)),
            pltpu.SemaphoreType.DMA((2,)),
        ],
        flops=2 * rows * par_dev * 256,
        data=2 * rows * par_dev,
        mib=32,
        after=after,
    )


def core_sum_kernel(idx, mine, peer, own, s1, s2, s3):
    y = idx[1]
    for k, ref in enumerate((own, s1, s2, s3)):
        at = pl.ds(pl.multiple_of(lax.rem(y + k, 4) * COLS, COLS), COLS)
        ref[...] = (mine[at, :] + peer[at, :]).astype(ref.dtype)


def core_sum(idx, mine, peer, after=()):
    rows = mine.shape[1]
    return call(
        core_sum_kernel,
        "core_sum",
        [shape((COLS, rows), F32)] + [shape((COLS, rows), BF)] * 3,
        [SMEM] + [VMEM] * 2,
        (idx, mine, peer),
        after=after,
    )


def info_kernel(idx, stations, decay, noise_scale, out):
    slot = idx[3] * 32 + idx[2] * 8 + idx[1] * 2 + idx[0]
    lane = lax.broadcasted_iota(jnp.int32, (1, 128), 1)
    rows = [
        stations[...].astype(F32),
        jnp.where(lane == slot, decay[0, 0], 0.0),
        jnp.where(lane == slot, noise_scale[0, 0], 0.0),
        jnp.zeros((2, 128), F32),
    ]
    out[...] = jnp.broadcast_to(jnp.concatenate(rows, axis=0)[None], out.shape)


def info(idx, stations, decay, noise_scale):
    return call(
        info_kernel,
        "info",
        shape((8, 8, 128), F32),
        [SMEM, VMEM, SMEM, SMEM],
        (idx, stations.reshape(4, 128), decay.reshape(1, 1), noise_scale.reshape(1, 1)),
    )


def params_kernel(table, sums):
    sums[...] = jnp.broadcast_to(jnp.sum(table[...], axis=0)[None], sums.shape)


def chain_kernel(table, near_h, ends_h, tops_h, hits, near, ends, tops, sem):
    held = []
    copies = []

    def send(src, dst, i):
        copies.append(pltpu.make_async_copy(src, dst, sem.at[i]))
        copies[-1].start()

    here = lax.broadcasted_iota(jnp.int32, (CH, CH), 0)
    there = lax.broadcasted_iota(jnp.int32, (CH, CH), 1)
    sid = lax.broadcasted_iota(jnp.int32, (128, CH), 0).astype(F32)
    n = hits.shape[1] // CH
    for b in range(n):
        at = slice(b * CH, (b + 1) * CH)
        r = (b % 2) * 2
        got = table[b // 2]
        row = jnp.concatenate([got[r : r + 1, :], got[r + 1 : r + 2, :]], axis=1)
        hit = jnp.broadcast_to(row, (128, CH)) == sid
        hit16 = jnp.where(hit, 1.0, 0.0).astype(BF)
        hits[:, at] = hit16
        same = lax.dot_general(hit16, hit16, TN, preferred_element_type=F32) > 0.5
        prior = jnp.max(jnp.where(same & (here < there), here, -1), axis=0, keepdims=True)
        later = jnp.min(jnp.where(same & (here > there), here, CH), axis=0, keepdims=True)
        near[b] = jnp.where((here == prior) | (here == later), 1.0, 0.0).astype(BF)
        ends[:128, at] = jnp.where(hit & (prior < 0), 1.0, 0.0).astype(BF)
        ends[128:, at] = jnp.where(hit & (later >= CH), 1.0, 0.0).astype(BF)
        held.append(jnp.max(jnp.where(hit, 1.0, 0.0), axis=1, keepdims=True))
        if b == n // 2 - 1:
            send(near.at[pl.ds(0, n // 2)], near_h.at[pl.ds(0, n // 2)], 0)
    send(near.at[pl.ds(n // 2, n // 2)], near_h.at[pl.ds(n // 2, n // 2)], 1)
    send(ends, ends_h, 2)
    before = jnp.zeros((128, 1), F32)
    after = jnp.zeros((128, 1), F32)
    for b in range(n):
        at = slice(b * CH, (b + 1) * CH)
        tops[:128, at] = (ends[:128, at].astype(F32) * (1.0 - before)).astype(BF)
        before = jnp.maximum(before, held[b])
        e = n - 1 - b
        at = slice(e * CH, (e + 1) * CH)
        tops[128:, at] = (ends[128:, at].astype(F32) * (1.0 - after)).astype(BF)
        after = jnp.maximum(after, held[e])
    send(tops, tops_h, 3)
    for copy in copies:
        copy.wait()


def chains(table, rows, after):
    n = rows // CH
    return call(
        chain_kernel,
        "chains",
        [pltpu.HBM((n, CH, CH), BF)] + [pltpu.HBM((256, rows), BF)] * 2 + [shape((128, rows), BF)],
        [VMEM],
        (table,),
        [pltpu.VMEM((n, CH, CH), BF)] + [pltpu.VMEM((256, rows), BF)] * 2 + [pltpu.SemaphoreType.DMA((4,))],
        data=12 * MB,
        after=after,
        out_specs=[HBM] * 3 + [VMEM],
    )


def coef_kernel(params, hits, coef, station):
    total = jnp.sum(params[...], axis=0)
    rate, level = total[4:5, :], total[5:6, :]
    scale = 1.0 / (level * level)
    rows = [(1.0 - rate * rate) * scale, rate * rate * scale, rate * scale]
    for i, row in enumerate(rows):
        station[i : i + 1, :] = row
    station[3:8, :] = jnp.zeros((5, 128), F32)
    split = []
    for row in rows:
        high = row.astype(BF)
        rest = row - high.astype(F32)
        mid = rest.astype(BF)
        split += [high, mid, (rest - mid.astype(F32)).astype(BF)]
    table = jnp.concatenate(split + [jnp.zeros((7, 128), BF)], axis=0)
    out = jnp.dot(table, hits[...], preferred_element_type=F32)
    for i in range(3):
        coef[i : i + 1, :] = out[3 * i : 3 * i + 1, :] + out[3 * i + 1 : 3 * i + 2, :] + out[3 * i + 2 : 3 * i + 3, :]
    coef[3:8, :] = jnp.zeros((5, coef.shape[1]), F32)


def coefs(params, hits):
    return call(
        coef_kernel,
        "coefs",
        [shape((8, hits.shape[1]), F32), shape((8, 128), F32)],
        [VMEM] * 2,
        (params, hits),
    )


def seen(v):
    return v[COLS : COLS + 1, :] > 0.5


def rows_kernel(own_h, r1_h, r2_h, r3_h, near_h, ends_h, coef, out, pay, *scratch):
    own, r1, r2, r3, near, ends, yaug, tips, carry, sem = scratch
    copies = [
        pltpu.make_async_copy(src, dst, sem.at[i])
        for i, (src, dst) in enumerate(
            ((own_h, own), (r1_h, r1), (r2_h, r2), (r3_h, r3), (ends_h, ends), (near_h, near))
        )
    ]
    for copy in copies:
        copy.start()
    for copy in copies[:4]:
        copy.wait()
    n = near.shape[0]
    total = own[...] + r1[...].astype(F32) + r2[...].astype(F32) + r3[...].astype(F32)
    yaug[:COLS, :] = total.astype(BF)
    yaug[COLS:, :] = jnp.ones((AUG - COLS, total.shape[1]), BF)
    copies[4].wait()
    spans = [slice(b * CH, (b + 1) * CH) for b in range(n)]
    for b in range(n):
        tips[b] = lax.dot_general(yaug[:, spans[b]], ends[:, spans[b]], NT, preferred_element_type=F32)
    below = jnp.zeros((AUG, 128), F32)
    above = jnp.zeros((AUG, 128), F32)
    for b in range(n):
        carry[b, :, :128] = below.astype(BF)
        here = tips[b, :, 128:]
        below = jnp.where(seen(here), here, below)
        e = n - 1 - b
        carry[e, :, 128:] = above.astype(BF)
        here = tips[e, :, :128]
        above = jnp.where(seen(here), here, above)
    tip = jnp.concatenate([above, below], axis=0).astype(BF)
    pay[...] = jnp.broadcast_to(tip[None], pay.shape)
    copies[5].wait()
    for b in range(n):
        y = yaug[:, spans[b]]
        around = jnp.dot(y, near[b], preferred_element_type=F32) + jnp.dot(
            carry[b], ends[:, spans[b]], preferred_element_type=F32
        )
        alpha = coef[0:1, spans[b]] + coef[1:2, spans[b]] * around[COLS : COLS + 1, :]
        out[:, spans[b]] = (
            alpha * y[:COLS, :].astype(F32) - coef[2:3, spans[b]] * around[:COLS, :]
        ).astype(BF)


def group_rows(own, recv, near, ends, coef):
    rows = own.shape[1]
    n = rows // CH
    return call(
        rows_kernel,
        "group_rows",
        [shape((COLS, rows), BF), shape((16, 2 * AUG, 128), BF)],
        [HBM] * 6 + [VMEM],
        (*map(hbm, (own, *recv, near, ends)), coef),
        [pltpu.VMEM((COLS, rows), F32)]
        + [pltpu.VMEM((COLS, rows), BF)] * 3
        + [pltpu.VMEM((n, CH, CH), BF), pltpu.VMEM((256, rows), BF)]
        + [pltpu.VMEM((AUG, rows), BF), pltpu.VMEM((n, AUG, 256), F32), pltpu.VMEM((n, AUG, 256), BF)]
        + [pltpu.SemaphoreType.DMA((6,))],
    )


def tie_kernel(idx, station, pay, out):
    me = idx[3] * 4 + idx[2]
    n = pay.shape[0]
    low = jnp.zeros((AUG, 128), F32)
    high = jnp.zeros((AUG, 128), F32)
    for j in range(n - 1):
        last = pay[j, AUG:, :].astype(F32)
        low = jnp.where(jnp.where(me > j, last[COLS : COLS + 1, :], 0.0) > 0.5, last, low)
        e = n - 1 - j
        first = pay[e, :AUG, :].astype(F32)
        high = jnp.where(jnp.where(me < e, first[COLS : COLS + 1, :], 0.0) > 0.5, first, high)
    square, rate = station[1:2, :], station[2:3, :]
    own = pay[me].astype(F32)
    for at, base, other in ((0, own[:AUG, :], low), (128, own[AUG:, :], high)):
        value = square * base[:COLS, :] - rate * other[:COLS, :]
        value = jnp.where(seen(base) & seen(other), value, 0.0).astype(BF)
        out[:, :, at : at + 128] = jnp.broadcast_to(value[None], (8, COLS, 128))


def tie(idx, station, pay, after):
    return call(
        tie_kernel, "tie", shape((8, COLS, 256), BF), [SMEM] + [VMEM] * 2, (idx, station, pay), after=after
    )


def panel_product(green, blocks, copies, panel, buf, own_blocks, acc, gate, sem, sem_blocks):
    steps = sem.shape[0]
    tile = buf.shape[0] // steps
    small = pltpu.make_async_copy(blocks, own_blocks, sem_blocks)
    small.start()
    for copy in copies:
        copy.start()
    for i in range(3):
        fetch(green, 0, buf, sem, i).start()
    small.wait()
    expand(own_blocks, gate)
    for copy in copies:
        copy.wait()
    for i in range(steps):
        fetch(green, 0, buf, sem, i).wait()
        if i + 3 < steps:
            fetch(green, 0, buf, sem, i + 3).start()
        mask_rows(buf, gate, i, tile, 0)
        at = slice(i * tile, (i + 1) * tile)
        part = jnp.dot(panel[:, at], buf[at, :], preferred_element_type=F32)
        acc[...] = part if i == 0 else acc[...] + part


def product_scratch(rows, par_dev, blocks):
    return [
        pltpu.VMEM((256, rows), BF),
        pltpu.VMEM((rows, par_dev), BF),
        pltpu.VMEM(blocks.shape, jnp.int32),
        pltpu.VMEM((256, par_dev), F32),
        pltpu.VMEM((rows // BLK, par_dev), F32),
        pltpu.SemaphoreType.DMA((8,)),
        pltpu.SemaphoreType.DMA((9,)),
    ]


def end_rows_kernel(green, blocks, tops, out, panel, buf, own_blocks, acc, gate, sem, sem2):
    copies = [pltpu.make_async_copy(tops, panel, sem2.at[0])]
    panel_product(green, blocks, copies, panel, buf, own_blocks, acc, gate, sem, sem2.at[8])
    out[...] = acc[...].astype(BF)


def end_rows(green, blocks, tops, after):
    rows, par_dev = green.shape
    return call(
        end_rows_kernel,
        "end_rows",
        shape((256, par_dev), BF),
        [HBM] * 3,
        tuple(map(hbm, (green, blocks, tops))),
        product_scratch(rows, par_dev, blocks),
        flops=2 * rows * par_dev * 256,
        data=2 * rows * par_dev,
        mib=32,
        after=after,
    )


def adjoint_kernel(idx, *refs):
    pieces, (green, blocks, out) = refs[:8], refs[8:11]
    panel, buf, own_blocks, acc, gate, sem, sem2 = refs[11:]
    core, y = idx[0], idx[1]
    copies = []
    for k in range(4):
        spot = lax.rem(y + 4 - k, 4) * COLS
        for base, j in ((core, k), (1 - core, 4 + k)):
            at = pl.ds(pl.multiple_of(base * 128 + spot, COLS), COLS)
            copies.append(pltpu.make_async_copy(pieces[j], panel.at[at, :], sem2.at[j]))
    panel_product(green, blocks, copies, panel, buf, own_blocks, acc, gate, sem, sem2.at[8])
    out[...] = acc[...]


def adjoint(idx, pieces, green, blocks, after=()):
    rows, par_dev = green.shape
    return call(
        adjoint_kernel,
        "adjoint",
        shape((256, par_dev), F32),
        [SMEM] + [HBM] * 10,
        (idx, *map(hbm, (*pieces, green, blocks))),
        product_scratch(rows, par_dev, blocks),
        flops=2 * rows * par_dev * 256,
        data=2 * rows * par_dev,
        mib=32,
        after=after,
    )


def finish_kernel(product, tied, rows_g, out, ties):
    for p in range(8):
        at = (p % 2) * 128 + (p // 2) * COLS
        ties[at : at + COLS, :] = tied[p]
    tile = 512
    for c in range(0, product.shape[1], tile):
        at = slice(c, c + tile)
        total = product[:, at] + jnp.dot(ties[...], rows_g[:, at], preferred_element_type=F32)
        out[:, :, at] = total.reshape(16, 16, tile).astype(BF)


def total_kernel(parts, out):
    total = parts[0].astype(F32)
    for j in range(1, parts.shape[0]):
        total = total + parts[j].astype(F32)
    out[...] = total


def y_shift(v, k):
    return lax.ppermute(v, "par", [(2 * y + c, 2 * ((y + k) % 4) + c) for y in range(4) for c in range(2)])


def core_swap(v):
    return lax.ppermute(v, "par", [(i, i ^ 1) for i in range(8)])


def x_shift(v, k):
    return lax.ppermute(v, "obs", [(4 * z + x, 4 * z + (x + k) % 4) for z in range(4) for x in range(4)])


def z_shift(v, k):
    return lax.ppermute(v, "obs", [(4 * z + x, 4 * ((z + k) % 4) + x) for z in range(4) for x in range(4)])


def exchange(v, axes):
    return lax.all_to_all(v, axes, split_axis=0, concat_axis=0, tiled=True)


def spread(shift, parts):
    got = {k: shift(parts[k - 1], k) for k in (2, 1, 3)}
    return [got[k] for k in (1, 2, 3)]


def local(green, blocks, probes, stations, decay, noise_scale):
    par = lax.axis_index("par")
    obs = lax.axis_index("obs")
    idx = jnp.stack([par % 2, par // 2, obs % 4, obs // 4]).astype(jnp.int32)
    blocks = blocks.T

    mail = info(idx, stations, decay, noise_scale)
    stations_g = exchange(mail, "par")
    mine, send = forward(idx, green, blocks, probes, after=(mail,))
    params = call(params_kernel, "params", shape((16, 8, 128), F32), [VMEM], (stations_g,), after=(send,))

    own, *sends = core_sum(idx, mine, core_swap(send), after=(params,))
    recv = spread(y_shift, sends)
    near, ends, tops, hits = chains(stations_g, green.shape[0], after=(own,))
    coef, station = coefs(exchange(params, "obs"), hits)

    rows_t, pay = group_rows(own, recv, near, ends, coef)
    pieces = [rows_t] + spread(y_shift, [rows_t] * 3)
    pay = exchange(pay, "obs")
    rows_g = end_rows(green, blocks, tops, after=(rows_t,))
    tied = tie(idx, station, pay, after=(rows_g,))
    pieces = pieces + [core_swap(p) for p in pieces]
    product = adjoint(idx, pieces, green, blocks, after=(tied,))
    tied = exchange(tied, "par")
    wide = green.shape[1]
    parts = call(
        finish_kernel,
        "finish",
        shape((16, 16, wide), BF),
        [VMEM] * 3,
        (product, tied, rows_g),
        [pltpu.VMEM((256, 256), BF)],
    )
    return call(total_kernel, "total", shape((16, wide), F32), [VMEM], (exchange(parts, "obs"),))


def solution(mesh):
    in_specs = (
        P("obs", "par"),
        P("obs", "par"),
        P("par", None),
        P(("obs", "par")),
        P(("obs", "par")),
        P(("obs", "par")),
    )
    out_specs = P("obs", "par")
    return jax.shard_map(local, mesh=mesh, in_specs=in_specs, out_specs=out_specs, check_vma=False)
```
